32 devices in a mesh: mem: 16 (over z, x, core), head: 2 (over y).
Axes of the slice: x: 2, y: 2, z: 4, core: 2. Of those that a mesh axis runs over, the one named last changes fastest.
Arguments:
- queries: bfloat16 [4096, 4096], P(('mem', 'head')), may hold values from -512 to 512
- local_keys: bfloat16 [4096, 1024], P(('mem', 'head')), may hold values from -6 to 6
- local_values: bfloat16 [4096, 1024], P(('mem', 'head')), may hold values from -12 to 12
- memory_keys: bfloat16 [65536, 1024], P('mem', 'head'), may hold values from -6 to 6
- memory_values: bfloat16 [65536, 1024], P('mem', 'head'), may hold values from -12 to 12
- block_ids: int32 [32, 8, 32], P('mem', 'head'), may hold values from 0 to 511, as said below
- mixing_offset_per_head: float32 [32], P('head'), may hold values from -2 to 2
Outputs:
- attended: bfloat16 [4096, 4096], P(('mem', 'head'))
The draws below stay inside these ranges and needn't reach their ends.
Inputs may be any that keep to these rules, and one draw needn't show every extreme that they name: Each row block_ids[b, h] names 32 different blocks. Over the 2 query blocks of one index of mem and one key-value head, the named blocks with one value of n // 32 are at most 4 different ones; for some value exactly 4, each named by all 2 of those query blocks.
All inputs are finite; a program needn't handle non-finite values.
Results may differ from the reference program's by a relative error of at most 0.0033.
Values may be sent and summed in bfloat16 or wider, within the bound.
A program may use at most 128 MiB of HBM per device.

```python
import math
import jax
import jax.numpy as jnp
from jax import lax

H = 32
KVH = 8
HD = 128
QB = 128
BL = 128
TOPK = 32
WINDOW = 256
SHARD_SPAN = 256
MB_DEV = 32
TOKENS = 4096
MBLOCKS = 512
MENTRIES = 65536
N_MEM = 16


def drawn_field(key, row_count, column_count, spread):
    field = jax.random.normal(jax.random.fold_in(key, 3), (row_count, column_count), jnp.float32)
    return jnp.clip(field, -6.0, 6.0) * spread


def drawn_keys(own_key, row_count):
    field = drawn_field(own_key, row_count, KVH * HD, 1.0)
    return field


def draw_local_keys(key, part):
    return drawn_keys(jax.random.fold_in(key, 21), TOKENS).astype(jnp.bfloat16)


def draw_memory_keys(key, part):
    return drawn_keys(jax.random.fold_in(key, 31), MENTRIES).astype(jnp.bfloat16)


def draw_queries(key, part):
    field = drawn_field(jax.random.fold_in(key, 41), TOKENS, H * HD, 2.0)
    return field.astype(jnp.bfloat16)


def draw_block_ids(key, part):
    block_rows = SHARD_SPAN // QB
    per_owner = (2 * TOPK + N_MEM - 1) // N_MEM
    width_all = N_MEM * per_owner
    pick_scores = jax.random.randint(jax.random.fold_in(key, 1), (N_MEM, KVH, N_MEM, MB_DEV), 0, 1 << 16)
    pick_scores = pick_scores * MB_DEV + jnp.arange(MB_DEV, dtype=jnp.int32)
    unused, picked = lax.top_k(pick_scores, per_owner)
    owners = jnp.arange(N_MEM, dtype=jnp.int32)
    candidates = (owners[:, None] * MB_DEV + picked).reshape(N_MEM, KVH, width_all)
    proposed_holder = jnp.repeat(owners, per_owner)
    heaviest_segment = jax.random.randint(jax.random.fold_in(key, 2), (KVH,), 0, N_MEM)
    center = jax.random.randint(jax.random.fold_in(key, 3), (N_MEM, KVH), 0, N_MEM)
    spacing_distance = jnp.abs(proposed_holder[None, None, :] - center[:, :, None])
    spacing_distance = jnp.minimum(spacing_distance, N_MEM - spacing_distance)
    closeness_measure = (N_MEM - spacing_distance) * 64 // N_MEM
    small_disturbance = jax.random.randint(jax.random.fold_in(key, 4), (N_MEM, block_rows, KVH, width_all), 0, 64)
    measure_addition = jnp.where(proposed_holder[None, :] == heaviest_segment[:, None], 1 << 12, 0)
    measure_grid_array = small_disturbance + closeness_measure[:, None, :, :] + measure_addition[None, None, :, :]
    measure_grid_array = measure_grid_array * width_all + jnp.arange(width_all, dtype=jnp.int32)
    unused_top, chosen = lax.top_k(measure_grid_array, TOPK)
    spread_cand = jnp.broadcast_to(candidates[:, None, :, :], (N_MEM, block_rows, KVH, width_all))
    chosen_ids = jnp.take_along_axis(spread_cand, chosen, axis=3)
    return chosen_ids.reshape(N_MEM * block_rows, KVH, TOPK).astype(jnp.int32)


def steps_of(key, extent, shards, least, largest):
    def one(axis_at, shards_of):
        steps = jax.random.uniform(jax.random.fold_in(jax.random.fold_in(key, 6), axis_at), (shards_of,), jnp.float32, least / len(shards), largest / len(shards))
        return jnp.repeat(jnp.exp(steps), extent[axis_at] // shards_of).reshape((-1,) + (1,) * (len(extent) - axis_at - 1))

    loudness = one(*shards[0])
    for cut in shards[1:]:
        loudness = loudness * one(*cut)
    return loudness


def centred(rng, extent, deviation, bound, shards=(), held_as=jnp.bfloat16):
    values = deviation * jax.random.normal(rng, extent, jnp.float32)
    if shards:
        values = values * steps_of(rng, extent, shards, -0.22, 0.18)
    return jnp.clip(values, -bound, bound).astype(held_as)


def setup_inputs(seed: int = 0) -> dict:
    splits = jax.random.split(jax.random.key(seed), 8)
    queries = draw_queries(jax.random.fold_in(splits[7], 71), 0)
    local_keys = draw_local_keys(jax.random.fold_in(splits[7], 71), 0)
    local_values = centred(splits[2], (TOKENS, KVH * HD), 2.0, 12.0, ((0, 32),))
    memory_keys = draw_memory_keys(jax.random.fold_in(splits[7], 71), 0)
    memory_values = centred(splits[4], (MENTRIES, KVH * HD), 2.0, 12.0, ((0, 16), (1, 2)))
    block_ids = draw_block_ids(jax.random.fold_in(splits[7], 71), 0)
    mixing_offset_per_head = jnp.clip(jax.random.uniform(splits[6], (H,), jnp.float32, -2.0, 2.0) * steps_of(splits[6], (H,), ((0, 2),), -0.4, 0.0), -2.0, 2.0)
    return {"queries": queries, "local_keys": local_keys, "local_values": local_values, "memory_keys": memory_keys, "memory_values": memory_values, "block_ids": block_ids, "mixing_offset_per_head": mixing_offset_per_head}


def attend_block(query_block, key_rows, value_rows, allowed):
    score_scale = 1.0 / math.sqrt(query_block.shape[-1])
    measure_grid_array = jnp.einsum('tgd,kd->tgk', query_block.astype(jnp.float32), key_rows.astype(jnp.float32), precision=lax.Precision.HIGHEST) * score_scale
    if allowed is not None:
        measure_grid_array = jnp.where(allowed[:, None, :], measure_grid_array, -1e+30)
    highest = lax.optimization_barrier(jnp.max(measure_grid_array, axis=2, keepdims=True))
    weights = jnp.exp(measure_grid_array - highest)
    denominator = lax.optimization_barrier(jnp.sum(weights, axis=2, keepdims=True))
    rounded = lax.optimization_barrier(weights.astype(jnp.bfloat16)).astype(jnp.float32)
    mixed = jnp.einsum('tgk,kd->tgd', rounded, value_rows.astype(jnp.float32), precision=lax.Precision.HIGHEST)
    return mixed / denominator

def reference(queries, local_keys, local_values, memory_keys, memory_values, block_ids, mixing_offset_per_head):
    group_size = H // KVH
    segment_count = TOKENS // QB
    span = WINDOW + QB
    query_grid = queries.reshape(segment_count, QB, KVH, group_size, HD)
    front = jnp.zeros((WINDOW, KVH * HD), local_keys.dtype)
    padded_keys = jnp.concatenate([front, local_keys], axis=0)
    padded_values = jnp.concatenate([front, local_values], axis=0)
    key_store = memory_keys.reshape(MBLOCKS, BL, KVH, HD)
    value_store = memory_values.reshape(MBLOCKS, BL, KVH, HD)
    gate_share = jax.nn.sigmoid(mixing_offset_per_head).reshape(KVH, group_size)

    def one_pair(couple_ordinal):
        block_index = (couple_ordinal // KVH).astype(jnp.int32)
        head_index = (couple_ordinal % KVH).astype(jnp.int32)
        zero = jnp.zeros((), jnp.int32)
        query_block = lax.dynamic_slice(query_grid, (block_index, zero, head_index, zero, zero), (1, QB, 1, group_size, HD)).reshape(QB, group_size, HD)
        start = (block_index * QB).astype(jnp.int32)
        key_rows = lax.dynamic_slice(padded_keys, (start, (head_index * HD).astype(jnp.int32)), (span, HD))
        value_rows = lax.dynamic_slice(padded_values, (start, (head_index * HD).astype(jnp.int32)), (span, HD))
        query_pos = start + jnp.arange(QB, dtype=jnp.int32)
        key_pos = start - WINDOW + jnp.arange(span, dtype=jnp.int32)
        spacing_distance = query_pos[:, None] - key_pos[None, :]
        allowed = (key_pos[None, :] >= 0) & (spacing_distance >= 0) & (spacing_distance < WINDOW)
        local_part = attend_block(query_block, key_rows, value_rows, allowed)
        chosen = block_ids[block_index, head_index]
        memory_key_rows = key_store[chosen, :, head_index, :].reshape(TOPK * BL, HD)
        memory_value_rows = value_store[chosen, :, head_index, :].reshape(TOPK * BL, HD)
        memory_part = attend_block(query_block, memory_key_rows, memory_value_rows, None)
        share = gate_share[head_index][None, :, None]
        return (share * memory_part + (1.0 - share) * local_part).astype(jnp.bfloat16)
    blended = lax.map(one_pair, jnp.arange(segment_count * KVH, dtype=jnp.int32))
    grid = blended.reshape(segment_count, KVH, QB, group_size, HD)
    return jnp.transpose(grid, (0, 2, 1, 3, 4)).reshape(TOKENS, H * HD)
```

```python
import functools
import math

import jax
import jax.numpy as jnp
from jax import lax
from jax.experimental import pallas as pl
from jax.experimental.pallas import tpu as pltpu
from jax.sharding import PartitionSpec as P

HD = 128
QB = 128
BL = 128
TOPK = 32
WINDOW = 256
LANES = 128
NONE = -1e30
SCALE2 = math.log2(math.e) / math.sqrt(HD)
VMEM_LIMIT = 56 * 1024 * 1024


def dot_t(a, b):
    return lax.dot_general(a, b, (((1,), (1,)), ((), ())), preferred_element_type=jnp.float32)


def lane_of(shape):
    return lax.broadcasted_iota(jnp.int32, shape, 1)


def split3(x):
    hi = x.astype(jnp.bfloat16).astype(jnp.float32)
    rest = x - hi
    mid = rest.astype(jnp.bfloat16).astype(jnp.float32)
    return hi, mid, rest - mid


def softmax_part(scores, values_and_ones):
    top = jnp.max(scores, axis=1, keepdims=True)
    weights = jnp.exp2((scores - top) * SCALE2).astype(jnp.bfloat16)
    both = jnp.dot(weights, values_and_ones, preferred_element_type=jnp.float32)
    return both[:, :HD], both[:, HD:], top


def part_kernel(group, half_heads, rows_per_chunk, cap, kv, sel, cnt, slots, q_ref, k_ref, v_ref, o_ref):
    chunk = 2 * pl.program_id(0) + sel[0]
    head = pl.program_id(1)
    col = pl.ds(pl.multiple_of(head * HD, HD), HD)
    width = (half_heads + 1) * HD

    @pl.when(head == 0)
    def _():
        for half in range(2):
            o_ref[0, :, half * width + half_heads * HD:(half + 1) * width] = jnp.zeros(
                (o_ref.shape[1], HD), jnp.bfloat16
            )

    def one_block(b, carry):
        pair = (chunk * rows_per_chunk + b) * kv + head
        rows = pl.ds(pl.multiple_of(b * QB, QB), QB)
        count = cnt[pair]

        def put(g, out, level):
            flat = head * group + g
            half = flat // half_heads
            at = flat - half * half_heads
            place = pl.multiple_of((flat + half) * HD, HD)
            o_ref[0, rows, pl.ds(place, HD)] = out.astype(jnp.bfloat16)
            stat = pl.ds(pl.multiple_of(half * width + half_heads * HD, HD), HD)
            lane = lane_of((QB, LANES))
            hi, mid, low = split3(level)
            old = o_ref[0, rows, stat].astype(jnp.float32)
            new = jnp.where(lane == at, hi, old)
            new = jnp.where(lane == at + 32, mid, new)
            new = jnp.where(lane == at + 64, low, new)
            o_ref[0, rows, stat] = new.astype(jnp.bfloat16)

        @pl.when(count == 0)
        def _():
            for g in range(group):
                put(g, jnp.zeros((QB, HD), jnp.float32), jnp.full((QB, LANES), NONE, jnp.float32))

        for size in range(1, cap + 1):
            @pl.when(count == size)
            def _(size=size):
                places = [
                    pl.ds(pl.multiple_of(slots[pair * cap + i] * BL, BL), BL) for i in range(size)
                ]
                keys = jnp.concatenate([k_ref[p, col] for p in places], axis=0)
                values = jnp.concatenate([v_ref[p, col] for p in places], axis=0)
                values = jnp.concatenate([values, jnp.ones_like(values)], axis=1)
                for g in range(group):
                    scores = dot_t(q_ref[rows, g * HD:(g + 1) * HD], keys)
                    out, total, top = softmax_part(scores, values)
                    put(g, out / total, top * SCALE2 + jnp.log2(total))

        return carry

    lax.fori_loop(0, rows_per_chunk, one_block, 0)


def memory_parts(sel, cnt, slots, queries, keys, values, chips, tokens, kv, group, cap):
    half_heads = kv * group // 2
    full = 2 * (half_heads + 1) * HD
    work = chips * tokens * kv * group * cap * BL // 2
    return pl.pallas_call(
        functools.partial(part_kernel, group, half_heads, tokens // QB, cap, kv),
        out_shape=jax.ShapeDtypeStruct((chips, tokens, full), jnp.bfloat16),
        grid_spec=pltpu.PrefetchScalarGridSpec(
            num_scalar_prefetch=3,
            grid=(chips, kv),
            in_specs=[
                pl.BlockSpec((tokens, group * HD), lambda c, h, s, n, t: (2 * c + s[0], h)),
                pl.BlockSpec(keys.shape, lambda c, h, s, n, t: (0, 0)),
                pl.BlockSpec(values.shape, lambda c, h, s, n, t: (0, 0)),
            ],
            out_specs=pl.BlockSpec((1, tokens, full), lambda c, h, s, n, t: (c, 0, 0)),
        ),
        compiler_params=pltpu.CompilerParams(vmem_limit_bytes=VMEM_LIMIT),
        cost_estimate=pl.CostEstimate(
            flops=work * HD * 6, bytes_accessed=chips * tokens * full * 4, transcendentals=work
        ),
        name="memory_parts",
    )(sel, cnt, slots, queries, keys, values)


def local_kernel(group, tokens, me, q_ref, k_ref, v_ref, o_ref):
    span = WINDOW + QB
    for b in range(tokens // QB):
        start = tokens + b * QB - WINDOW
        keys = k_ref[start:start + span, :]
        values = v_ref[start:start + span, :]
        values = jnp.concatenate([values, jnp.ones_like(values)], axis=1)
        rows = slice(b * QB, (b + 1) * QB)
        q_at = b * QB + lax.broadcasted_iota(jnp.int32, (QB, span), 0)
        k_at = start - tokens + lax.broadcasted_iota(jnp.int32, (QB, span), 1)
        gap = q_at - k_at
        allowed = (k_at + me[0] * tokens >= 0) & (gap >= 0) & (gap < WINDOW)
        for g in range(group):
            scores = dot_t(q_ref[rows, g * HD:(g + 1) * HD], keys)
            out, total, _ = softmax_part(jnp.where(allowed, scores, NONE), values)
            o_ref[rows, g * HD:(g + 1) * HD] = out / total


def local_part(me, queries, keys, values, kv, group):
    tokens = queries.shape[0]
    return pl.pallas_call(
        functools.partial(local_kernel, group, tokens),
        out_shape=jax.ShapeDtypeStruct(queries.shape, jnp.float32),
        grid_spec=pltpu.PrefetchScalarGridSpec(
            num_scalar_prefetch=1,
            grid=(kv,),
            in_specs=[
                pl.BlockSpec((tokens, group * HD), lambda h, m: (0, h)),
                pl.BlockSpec((keys.shape[0], HD), lambda h, m: (0, h)),
                pl.BlockSpec((keys.shape[0], HD), lambda h, m: (0, h)),
            ],
            out_specs=pl.BlockSpec((tokens, group * HD), lambda h, m: (0, h)),
        ),
        compiler_params=pltpu.CompilerParams(vmem_limit_bytes=VMEM_LIMIT),
        cost_estimate=pl.CostEstimate(
            flops=tokens * kv * group * 384 * HD * 6,
            bytes_accessed=tokens * kv * group * HD * 6,
            transcendentals=tokens * kv * group * 384,
        ),
        name="local_part",
    )(me, queries, keys, values)


def level_of(tile):
    x = tile.astype(jnp.float32)
    return x + pltpu.roll(x, LANES - 32, 1) + pltpu.roll(x, LANES - 64, 1)


def merge_half(half_heads, parts):
    levels = [level_of(part[:, half_heads * HD:]) for part in parts]
    top = functools.reduce(jnp.maximum, levels)
    weights = [jnp.exp2(level - top) for level in levels]
    total = functools.reduce(jnp.add, weights)
    shares = [w / total for w in weights]
    outs = []
    for at in range(half_heads):
        cols = slice(at * HD, (at + 1) * HD)
        outs.append(
            functools.reduce(
                jnp.add,
                [
                    part[:, cols].astype(jnp.float32) * share[:, at:at + 1]
                    for part, share in zip(parts, shares)
                ],
            )
        )
    return outs, top + jnp.log2(total)


def merge_kernel(half_heads, with_received, places, *refs):
    count = 6 if with_received else 4
    ins, outs = refs[:count], refs[count:]
    for half in range(2):
        parts = [ins[half][0], ins[2 + half][0]]
        if with_received:
            parts.append(ins[4 + half][...])
        merged, level = merge_half(half_heads, parts)
        for at, out in enumerate(merged):
            outs[half][:, at * HD:(at + 1) * HD] = out.astype(jnp.bfloat16)
        lane = lane_of(level.shape)
        hi, mid, low = split3(level)
        stat = jnp.where(lane < 32, hi, 0.0)
        stat = jnp.where((lane >= 32) & (lane < 64), pltpu.roll(mid, 32, 1), stat)
        stat = jnp.where((lane >= 64) & (lane < 96), pltpu.roll(low, 64, 1), stat)
        outs[half][:, half_heads * HD:] = stat.astype(jnp.bfloat16)


def final_kernel(half_heads, places, *refs):
    ins, local_ref, gate_ref, o_ref = refs[:6], refs[6], refs[7], refs[8]
    for half in range(2):
        parts = [ins[half][0], ins[2 + half][0], ins[4 + half][...]]
        merged, _ = merge_half(half_heads, parts)
        for at, out in enumerate(merged):
            flat = half * half_heads + at
            cols = slice(flat * HD, (flat + 1) * HD)
            share = gate_ref[:, cols]
            o_ref[:, cols] = (share * out + (1.0 - share) * local_ref[:, cols]).astype(jnp.bfloat16)


def merge_step(places, own, sib, received, half_heads, local=None, gate=None):
    tokens = own.shape[1]
    width = (half_heads + 1) * HD
    rows = QB // 2
    part_specs = [
        pl.BlockSpec((1, rows, width), lambda r, p: (p[0], r, 0)),
        pl.BlockSpec((1, rows, width), lambda r, p: (p[1], r, 1)),
    ]
    flat_spec = pl.BlockSpec((rows, width), lambda r, p: (r, 0))
    in_specs = part_specs * 2
    operands = [own, own, sib, sib]
    if received is not None:
        in_specs = in_specs + [flat_spec] * 2
        operands += list(received)
    if local is None:
        kernel = functools.partial(merge_kernel, half_heads, received is not None)
        out_shape = [jax.ShapeDtypeStruct((tokens, width), jnp.bfloat16)] * 2
        out_specs = [flat_spec] * 2
    else:
        kernel = functools.partial(final_kernel, half_heads)
        full = 2 * half_heads * HD
        wide = pl.BlockSpec((rows, full), lambda r, p: (r, 0))
        in_specs = in_specs + [wide, pl.BlockSpec((1, full), lambda r, p: (0, 0))]
        operands += [local, gate]
        out_shape = jax.ShapeDtypeStruct((tokens, full), jnp.bfloat16)
        out_specs = wide
    return pl.pallas_call(
        kernel,
        out_shape=out_shape,
        grid_spec=pltpu.PrefetchScalarGridSpec(
            num_scalar_prefetch=1, grid=(tokens // rows,), in_specs=in_specs, out_specs=out_specs
        ),
        compiler_params=pltpu.CompilerParams(vmem_limit_bytes=VMEM_LIMIT),
        name="merge_step" if local is None else "merge_last",
    )(places, *operands)


def chip_ring(chips):
    across = 1
    while across * 2 * across * 2 <= chips:
        across *= 2
    deep = chips // across
    walk = []
    for z in range(deep):
        row = range(1, across) if z % 2 == 0 else range(across - 1, 0, -1)
        walk += [z * across + x for x in row]
    return walk + [z * across for z in range(deep - 1, -1, -1)]


def block_tables(block_ids, first, blocks_here, cap):
    local = block_ids - first
    mine = (local >= 0) & (local < blocks_here)
    rank = jnp.cumsum(mine.astype(jnp.int32), axis=-1) - 1
    slots = [
        jnp.sum(jnp.where(mine & (rank == i), local, 0), axis=-1, dtype=jnp.int32)
        for i in range(cap)
    ]
    count = jnp.sum(mine, axis=-1, dtype=jnp.int32)
    return count.reshape(-1), jnp.stack(slots, axis=-1).reshape(-1)


def per_device(
    queries, local_keys, local_values, memory_keys, memory_values, block_ids, mixing_offset_per_head
):
    devices = lax.axis_size("mem")
    me = lax.axis_index("mem")
    chips = devices // 2
    core = me % 2
    q_heads, keys_own, values_own = (
        lax.all_to_all(x, "head", split_axis=1, concat_axis=0, tiled=True)
        for x in (queries, local_keys, local_values)
    )
    tokens = q_heads.shape[0]
    kv = keys_own.shape[1] // HD
    group = q_heads.shape[1] // (kv * HD)
    half_heads = kv * group // 2
    blocks_here = memory_keys.shape[0] // BL
    cap = (2 * TOPK + devices - 1) // devices

    all_ids = lax.all_gather(block_ids, "mem", axis=0, tiled=True)
    all_queries = lax.all_gather(q_heads, "mem", axis=0, tiled=True)
    cnt, slots = block_tables(all_ids, me * blocks_here, blocks_here, cap)

    behind = [(i, i + 1) for i in range(devices - 1)]
    keys_before, values_before = (lax.ppermute(x, "mem", behind) for x in (keys_own, values_own))
    local_out = local_part(
        me.reshape(1).astype(jnp.int32),
        q_heads,
        jnp.concatenate([keys_before, keys_own], axis=0),
        jnp.concatenate([values_before, values_own], axis=0),
        kv,
        group,
    )
    gate = jnp.repeat(jax.nn.sigmoid(mixing_offset_per_head), HD)[None, :]

    def parts_for(which, cnt):
        return memory_parts(
            which.reshape(1).astype(jnp.int32), cnt, slots, all_queries, memory_keys, memory_values,
            chips, tokens, kv, group, cap,
        )

    siblings = [(i, i ^ 1) for i in range(devices)]
    sib = lax.ppermute(parts_for(1 - core, cnt), "mem", siblings)
    if kv == 1:
        sib, cnt = lax.optimization_barrier((sib, cnt))
    own = parts_for(core, cnt)

    ring = chip_ring(chips)
    order = jnp.array(ring, jnp.int32)
    position = jnp.array([ring.index(c) for c in range(chips)], jnp.int32)[me // 2]
    onward = [
        (ring[i] * 2 + c, ring[(i + 1) % chips] * 2 + c) for i in range(chips) for c in range(2)
    ]
    backward = [(b, a) for a, b in onward]

    received = None
    for step in range(1, chips + 1):
        places = jnp.stack([order[(position - step) % chips], order[(position + step) % chips]])
        if step == chips:
            break
        right, left = merge_step(places, own, sib, received, half_heads)
        received = (
            lax.ppermute(right, "mem", onward),
            lax.ppermute(left, "mem", backward),
        )
    blended = merge_step(places, own, sib, received, half_heads, local_out, gate)
    return lax.all_to_all(blended, "head", split_axis=0, concat_axis=1, tiled=True)


def solution(mesh):
    return jax.shard_map(
        per_device,
        mesh=mesh,
        in_specs=(
            P(("mem", "head"), None),
            P(("mem", "head"), None),
            P(("mem", "head"), None),
            P("mem", "head"),
            P("mem", "head"),
            P("mem", "head", None),
            P("head"),
        ),
        out_specs=P(("mem", "head"), None),
        check_vma=False,
    )
```

```python
import functools
import math

import jax
import jax.numpy as jnp
from jax import lax
from jax.experimental import pallas as pl
from jax.experimental.pallas import tpu as pltpu
from jax.sharding import PartitionSpec as P

HD = 128
QB = 128
BL = 128
TOPK = 32
WINDOW = 256
LANES = 128
NONE = -1e30
SCALE2 = math.log2(math.e) / math.sqrt(HD)
VMEM_LIMIT = 56 * 1024 * 1024


def dot_t(a, b):
    return lax.dot_general(a, b, (((1,), (1,)), ((), ())), preferred_element_type=jnp.float32)


def lane_of(shape):
    return lax.broadcasted_iota(jnp.int32, shape, 1)


def split3(x):
    hi = x.astype(jnp.bfloat16).astype(jnp.float32)
    rest = x - hi
    mid = rest.astype(jnp.bfloat16).astype(jnp.float32)
    return hi, mid, rest - mid


def packed_level(level):
    lane = lane_of(level.shape)
    hi, mid, low = split3(level)
    stat = jnp.where(lane < 32, hi, 0.0)
    stat = jnp.where((lane >= 32) & (lane < 64), pltpu.roll(mid, 32, 1), stat)
    stat = jnp.where((lane >= 64) & (lane < 96), pltpu.roll(low, 64, 1), stat)
    return stat.astype(jnp.bfloat16)


def softmax_part(scores, values_and_ones):
    top = jnp.max(scores, axis=1, keepdims=True)
    weights = jnp.exp2((scores - top) * SCALE2).astype(jnp.bfloat16)
    both = jnp.dot(weights, values_and_ones, preferred_element_type=jnp.float32)
    return both[:, :HD], both[:, HD:], top


def part_kernel(step, group, cap, kv, first, per_kv, dests, cnt, slots, q_ref, k_ref, v_ref, o_ref, top_ref, total_ref):
    index = pl.program_id(0)
    chunk = dests[step]
    tokens = q_ref.shape[0]
    kv_head = (first + index * group) // per_kv

    def one_block(b, carry):
        pair = (chunk * (tokens // QB) + b) * kv + kv_head
        rows = pl.ds(pl.multiple_of(b * QB, QB), QB)
        count = cnt[pair]
        lane = lane_of((QB, LANES))

        def put(outs, totals, tops):
            top, total = top_ref[rows, :], total_ref[rows, :]
            for g in range(group):
                o_ref[rows, pl.ds(pl.multiple_of((index * group + g) * HD, HD), HD)] = outs[g].astype(
                    jnp.bfloat16
                )
                here = lane == index * group + g
                top = jnp.where(here, tops[g], top)
                total = jnp.where(here, totals[g], total)
            top_ref[rows, :] = top
            total_ref[rows, :] = total

        @pl.when(count == 0)
        def _():
            blank = jnp.zeros((QB, HD), jnp.float32)
            put([blank] * group, [blank + 1.0] * group, [blank + NONE] * group)

        for size in range(1, cap + 1):
            @pl.when(count == size)
            def _(size=size):
                places = [
                    pl.ds(pl.multiple_of(slots[pair * cap + i] * BL, BL), BL) for i in range(size)
                ]
                keys = jnp.concatenate([k_ref[p, :] for p in places], axis=0)
                values = jnp.concatenate([v_ref[p, :] for p in places], axis=0)
                values = jnp.concatenate([values, jnp.ones_like(values)], axis=1)
                asked = jnp.concatenate(
                    [q_ref[rows, g * HD:(g + 1) * HD] for g in range(group)], axis=0
                )
                out, total, top = softmax_part(dot_t(asked, keys), values)
                out = out / total
                cut = [slice(g * QB, (g + 1) * QB) for g in range(group)]
                put([out[c] for c in cut], [total[c] for c in cut], [top[c] for c in cut])

        return carry

    lax.fori_loop(0, tokens // QB, one_block, 0)

    @pl.when(index == pl.num_programs(0) - 1)
    def _():
        o_ref[:, -LANES:] = packed_level(top_ref[...] * SCALE2 + jnp.log2(total_ref[...]))


def memory_part(step, dests, cnt, slots, queries, keys, values, kv, all_heads, first, cap):
    tokens, width = queries.shape
    heads = width // HD
    per_kv = all_heads // kv
    group = min(per_kv, heads)
    work = tokens * heads * cap * BL // 2
    return pl.pallas_call(
        functools.partial(part_kernel, step, group, cap, kv, first, per_kv),
        out_shape=jax.ShapeDtypeStruct((tokens, width + LANES), jnp.bfloat16),
        grid_spec=pltpu.PrefetchScalarGridSpec(
            num_scalar_prefetch=3,
            grid=(heads // group,),
            in_specs=[
                pl.BlockSpec((tokens, group * HD), lambda i, d, n, t: (0, i)),
                pl.BlockSpec((keys.shape[0], HD), lambda i, d, n, t: (0, (first + i * group) // per_kv)),
                pl.BlockSpec((keys.shape[0], HD), lambda i, d, n, t: (0, (first + i * group) // per_kv)),
            ],
            out_specs=pl.BlockSpec((tokens, width + LANES), lambda i, d, n, t: (0, 0)),
            scratch_shapes=[pltpu.VMEM((tokens, LANES), jnp.float32)] * 2,
        ),
        compiler_params=pltpu.CompilerParams(vmem_limit_bytes=VMEM_LIMIT),
        cost_estimate=pl.CostEstimate(
            flops=work * HD * 12, bytes_accessed=keys.size * 2, transcendentals=work
        ),
        name="memory_part",
    )(dests, cnt, slots, queries, keys, values)


def local_kernel(group, tokens, me, q_ref, k_ref, v_ref, o_ref):
    span = WINDOW + QB
    for b in range(tokens // QB):
        start = tokens + b * QB - WINDOW
        keys = k_ref[start:start + span, :]
        values = v_ref[start:start + span, :]
        values = jnp.concatenate([values, jnp.ones_like(values)], axis=1)
        rows = slice(b * QB, (b + 1) * QB)
        q_at = b * QB + lax.broadcasted_iota(jnp.int32, (QB, span), 0)
        k_at = start - tokens + lax.broadcasted_iota(jnp.int32, (QB, span), 1)
        gap = q_at - k_at
        allowed = (k_at + me[0] * tokens >= 0) & (gap >= 0) & (gap < WINDOW)
        for g in range(group):
            scores = dot_t(q_ref[rows, g * HD:(g + 1) * HD], keys)
            out, total, _ = softmax_part(jnp.where(allowed, scores, NONE), values)
            o_ref[rows, g * HD:(g + 1) * HD] = out / total


def local_part(me, queries, keys, values, kv, group):
    tokens = queries.shape[0]
    return pl.pallas_call(
        functools.partial(local_kernel, group, tokens),
        out_shape=jax.ShapeDtypeStruct(queries.shape, jnp.float32),
        grid_spec=pltpu.PrefetchScalarGridSpec(
            num_scalar_prefetch=1,
            grid=(kv,),
            in_specs=[
                pl.BlockSpec((tokens, group * HD), lambda h, m: (0, h)),
                pl.BlockSpec((keys.shape[0], HD), lambda h, m: (0, h)),
                pl.BlockSpec((keys.shape[0], HD), lambda h, m: (0, h)),
            ],
            out_specs=pl.BlockSpec((tokens, group * HD), lambda h, m: (0, h)),
        ),
        compiler_params=pltpu.CompilerParams(vmem_limit_bytes=VMEM_LIMIT),
        cost_estimate=pl.CostEstimate(
            flops=tokens * kv * group * 384 * HD * 6,
            bytes_accessed=tokens * kv * group * HD * 6,
            transcendentals=tokens * kv * group * 384,
        ),
        name="local_part",
    )(me, queries, keys, values)


def level_of(tile):
    x = tile.astype(jnp.float32)
    return x + pltpu.roll(x, LANES - 32, 1) + pltpu.roll(x, LANES - 64, 1)


def merged(parts):
    heads = parts[0].shape[1] // HD - 1
    levels = [level_of(part[:, heads * HD:]) for part in parts]
    top = functools.reduce(jnp.maximum, levels)
    weights = [jnp.exp2(level - top) for level in levels]
    total = functools.reduce(jnp.add, weights)
    shares = [w / total for w in weights]
    outs = []
    for at in range(heads):
        cols = slice(at * HD, (at + 1) * HD)
        terms = [
            part[:, cols].astype(jnp.float32) * share[:, at:at + 1]
            for part, share in zip(parts, shares)
        ]
        outs.append(functools.reduce(jnp.add, terms))
    return outs, top + jnp.log2(total)


def merge_kernel(part_ref, received_ref, o_ref):
    outs, level = merged([part_ref, received_ref])
    for at, out in enumerate(outs):
        o_ref[:, at * HD:(at + 1) * HD] = out.astype(jnp.bfloat16)
    o_ref[:, -LANES:] = packed_level(level)


def final_kernel(right_ref, right_got, left_ref, left_got, local_ref, gate_ref, o_ref):
    outs = merged([right_ref, right_got])[0] + merged([left_ref, left_got])[0]
    for at, out in enumerate(outs):
        cols = slice(at * HD, (at + 1) * HD)
        share = gate_ref[:, cols]
        o_ref[:, cols] = (share * out + (1.0 - share) * local_ref[:, cols]).astype(jnp.bfloat16)


def merge(part, received):
    tokens, width = part.shape
    rows = QB // 2
    spec = pl.BlockSpec((rows, width), lambda r: (r, 0))
    return pl.pallas_call(
        merge_kernel,
        out_shape=jax.ShapeDtypeStruct(part.shape, jnp.bfloat16),
        grid=(tokens // rows,),
        in_specs=[spec] * 2,
        out_specs=spec,
        cost_estimate=pl.CostEstimate(
            flops=part.size * 8, bytes_accessed=part.size * 6, transcendentals=tokens * LANES * 4
        ),
        name="merge",
    )(part, received)


def finish(right, right_got, left, left_got, local, gate):
    tokens, width = right.shape
    rows = QB // 2
    full = local.shape[1]
    spec = pl.BlockSpec((rows, width), lambda r: (r, 0))
    wide = pl.BlockSpec((rows, full), lambda r: (r, 0))
    return pl.pallas_call(
        final_kernel,
        out_shape=jax.ShapeDtypeStruct((tokens, full), jnp.bfloat16),
        grid=(tokens // rows,),
        in_specs=[spec] * 4 + [wide, pl.BlockSpec((1, full), lambda r: (0, 0))],
        out_specs=wide,
        name="finish",
    )(right, right_got, left, left_got, local, gate)


def chip_ring(chips):
    across = 1
    while across * 2 * across * 2 <= chips:
        across *= 2
    deep = chips // across
    walk = []
    for z in range(deep):
        row = range(1, across) if z % 2 == 0 else range(across - 1, 0, -1)
        walk += [z * across + x for x in row]
    return walk + [z * across for z in range(deep - 1, -1, -1)]


def block_tables(block_ids, first, blocks_here, cap):
    local = block_ids - first
    mine = (local >= 0) & (local < blocks_here)
    rank = jnp.cumsum(mine.astype(jnp.int32), axis=-1) - 1
    slots = [
        jnp.sum(jnp.where(mine & (rank == i), local, 0), axis=-1, dtype=jnp.int32)
        for i in range(cap)
    ]
    count = jnp.sum(mine, axis=-1, dtype=jnp.int32)
    return count.reshape(-1), jnp.stack(slots, axis=-1).reshape(-1)


def per_device(
    queries, local_keys, local_values, memory_keys, memory_values, block_ids, mixing_offset_per_head
):
    devices = lax.axis_size("mem")
    me = lax.axis_index("mem")
    chips = devices // 2
    chip, core = me // 2, me % 2
    pairs = [[2 * c, 2 * c + 1] for c in range(chips)]
    chip_keys, chip_values = (
        lax.all_gather(x, "mem", axis=0, tiled=True, axis_index_groups=pairs)
        for x in (memory_keys, memory_values)
    )
    all_ids = lax.all_gather(block_ids, "mem", axis=0, tiled=True)
    q_heads, keys_own, values_own = (
        lax.all_to_all(x, "head", split_axis=1, concat_axis=0, tiled=True)
        for x in (queries, local_keys, local_values)
    )
    tokens = q_heads.shape[0]
    kv = keys_own.shape[1] // HD
    heads = q_heads.shape[1] // HD
    group = heads // kv
    half = heads // 2
    blocks_here = chip_keys.shape[0] // BL
    cap = 2 * ((2 * TOPK + devices - 1) // devices)
    cnt, slots = block_tables(all_ids, chip * blocks_here, blocks_here, cap)

    ring = chip_ring(chips)
    order = jnp.array(ring, jnp.int32)
    position = jnp.array([ring.index(c) for c in range(chips)], jnp.int32)[chip]
    steps = jnp.arange(chips, dtype=jnp.int32)
    from_left = order[(position - steps) % chips] * 2 + core
    from_right = order[(position + steps) % chips] * 2 + core
    onward = [
        (ring[i] * 2 + c, ring[(i + 1) % chips] * 2 + c) for i in range(chips) for c in range(2)
    ]
    backward = [(b, a) for a, b in onward]

    def part(step, asked, dests, first):
        return memory_part(
            step, dests, cnt, slots, asked, chip_keys, chip_values, kv, heads, first, cap
        )

    right, left = q_heads[:, :half * HD], q_heads[:, half * HD:]
    own_right, own_left = part(0, right, from_left, 0), part(0, left, from_right, half)

    behind = [(i, i + 1) for i in range(devices - 1)]
    keys_before, values_before = (lax.ppermute(x, "mem", behind) for x in (keys_own, values_own))
    local_out = local_part(
        me.reshape(1).astype(jnp.int32),
        q_heads,
        jnp.concatenate([keys_before, keys_own], axis=0),
        jnp.concatenate([values_before, values_own], axis=0),
        kv,
        group,
    )
    gate = jnp.repeat(jax.nn.sigmoid(mixing_offset_per_head), HD)[None, :]

    got_right = got_left = None
    for step in range(1, chips):
        right = lax.ppermute(right, "mem", onward)
        left = lax.ppermute(left, "mem", backward)
        part_right = part(step, right, from_left, 0)
        part_left = part(step, left, from_right, half)
        if step > 1:
            part_right = merge(part_right, got_right)
            part_left = merge(part_left, got_left)
        got_right = lax.ppermute(part_right, "mem", onward)
        got_left = lax.ppermute(part_left, "mem", backward)
    blended = finish(own_right, got_right, own_left, got_left, local_out, gate)
    return lax.all_to_all(blended, "head", split_axis=0, concat_axis=1, tiled=True)


def solution(mesh):
    return jax.shard_map(
        per_device,
        mesh=mesh,
        in_specs=(
            P(("mem", "head"), None),
            P(("mem", "head"), None),
            P(("mem", "head"), None),
            P("mem", "head"),
            P("mem", "head"),
            P("mem", "head", None),
            P("head"),
        ),
        out_specs=P(("mem", "head"), None),
        check_vma=False,
    )
```

```python
import functools
import math

import jax
import jax.numpy as jnp
from jax import lax
from jax.experimental import pallas as pl
from jax.experimental.pallas import tpu as pltpu
from jax.sharding import PartitionSpec as P

HD = 128
QB = 128
BL = 128
TOPK = 32
WINDOW = 256
LANES = 128
NONE = -1e30
SCALE2 = math.log2(math.e) / math.sqrt(HD)
VMEM_LIMIT = 28 * 1024 * 1024


def dot_t(a, b):
    return lax.dot_general(a, b, (((1,), (1,)), ((), ())), preferred_element_type=jnp.float32)


def lane_of(shape):
    return lax.broadcasted_iota(jnp.int32, shape, 1)


def split3(x):
    hi = x.astype(jnp.bfloat16).astype(jnp.float32)
    rest = x - hi
    mid = rest.astype(jnp.bfloat16).astype(jnp.float32)
    return hi, mid, rest - mid


def packed_level(level):
    lane = lane_of(level.shape)
    hi, mid, low = split3(level)
    stat = jnp.where(lane < 32, hi, 0.0)
    stat = jnp.where((lane >= 32) & (lane < 64), pltpu.roll(mid, 32, 1), stat)
    stat = jnp.where((lane >= 64) & (lane < 96), pltpu.roll(low, 64, 1), stat)
    return stat.astype(jnp.bfloat16)


def softmax_part(scores, values_and_ones):
    top = jnp.max(scores, axis=1, keepdims=True)
    weights = jnp.exp2((scores - top) * SCALE2).astype(jnp.bfloat16)
    both = jnp.dot(weights, values_and_ones, preferred_element_type=jnp.float32)
    return both[:, :HD], both[:, HD:], top


def part_kernel(
    step, chips, group, cap, kv, per_kv, dests, table, right_ref, left_ref, k_ref, k_sib, v_ref, v_sib,
    o_ref, q_ref, top_ref, total_ref
):
    index = pl.program_id(0)
    each = pl.num_programs(0) // 2
    way = index // each
    chunk = dests[way * chips + step]
    tokens = q_ref.shape[0]
    blocks = k_ref.shape[0] // BL
    kv_head = index * group // per_kv
    place0 = index * group + way

    @pl.when(way == 0)
    def _():
        q_ref[...] = right_ref[...]

    @pl.when(way == 1)
    def _():
        q_ref[...] = left_ref[...]

    def one_block(b, carry):
        entry = ((chunk * (tokens // QB) + b) * kv + kv_head) * (1 + cap)
        rows = pl.ds(pl.multiple_of(b * QB, QB), QB)
        count = table[entry]
        lane = lane_of((QB, LANES))

        def put(outs, totals, tops):
            top, total = top_ref[rows, :], total_ref[rows, :]
            for g in range(group):
                o_ref[rows, pl.ds(pl.multiple_of((place0 + g) * HD, HD), HD)] = outs[g].astype(
                    jnp.bfloat16
                )
                here = lane == (index - way * each) * group + g
                top = jnp.where(here, tops[g], top)
                total = jnp.where(here, totals[g], total)
            top_ref[rows, :] = top
            total_ref[rows, :] = total

        def block_of(own, sib, i):
            slot = table[entry + 1 + i]
            inside = pl.multiple_of(lax.rem(slot, blocks) * BL, BL)
            return jnp.where(slot < blocks, own[pl.ds(inside, BL), :], sib[pl.ds(inside, BL), :])

        @pl.when(count == 0)
        def _():
            blank = jnp.zeros((QB, HD), jnp.float32)
            put([blank] * group, [blank + 1.0] * group, [blank + NONE] * group)

        for size in range(1, cap + 1):
            @pl.when(count == size)
            def _(size=size):
                keys = jnp.concatenate([block_of(k_ref, k_sib, i) for i in range(size)], axis=0)
                values = jnp.concatenate([block_of(v_ref, v_sib, i) for i in range(size)], axis=0)
                values = jnp.concatenate([values, jnp.ones_like(values)], axis=1)
                asked = jnp.concatenate(
                    [q_ref[rows, g * HD:(g + 1) * HD] for g in range(group)], axis=0
                )
                out, total, top = softmax_part(dot_t(asked, keys), values)
                out = out / total
                cut = [slice(g * QB, (g + 1) * QB) for g in range(group)]
                put([out[c] for c in cut], [total[c] for c in cut], [top[c] for c in cut])

        return carry

    lax.fori_loop(0, tokens // QB, one_block, 0)

    @pl.when(index == (way + 1) * each - 1)
    def _():
        stat = pl.ds(pl.multiple_of((place0 + group) * HD, HD), HD)
        o_ref[:, stat] = packed_level(top_ref[...] * SCALE2 + jnp.log2(total_ref[...]))


def memory_part(step, dests, table, right, left, keys, values, kv, cap):
    tokens, width = right.shape
    heads = width // HD
    per_kv = 2 * heads // kv
    group = min(per_kv, heads)
    each = heads // group
    chips = dests.shape[0] // 2
    work = 2 * tokens * heads * cap * BL // 2
    of_head = pl.BlockSpec((keys[0].shape[0], HD), lambda i, d, t: (0, i * group // per_kv))
    return pl.pallas_call(
        functools.partial(part_kernel, step, chips, group, cap, kv, per_kv),
        out_shape=jax.ShapeDtypeStruct((tokens, 2 * (width + LANES)), jnp.bfloat16),
        grid_spec=pltpu.PrefetchScalarGridSpec(
            num_scalar_prefetch=2,
            grid=(2 * each,),
            in_specs=[
                pl.BlockSpec((tokens, group * HD), lambda i, d, t: (0, jnp.minimum(i, each - 1))),
                pl.BlockSpec((tokens, group * HD), lambda i, d, t: (0, jnp.maximum(i - each, 0))),
            ] + [of_head] * 4,
            out_specs=pl.BlockSpec((tokens, 2 * (width + LANES)), lambda i, d, t: (0, 0)),
            scratch_shapes=[pltpu.VMEM((tokens, group * HD), jnp.bfloat16)]
            + [pltpu.VMEM((tokens, LANES), jnp.float32)] * 2,
        ),
        compiler_params=pltpu.CompilerParams(vmem_limit_bytes=VMEM_LIMIT),
        cost_estimate=pl.CostEstimate(
            flops=work * HD * 6, bytes_accessed=keys[0].size * 8, transcendentals=work
        ),
        name="memory_part",
    )(dests, table, right, left, *keys, *values)


def local_kernel(group, tokens, me, q_ref, k_ref, v_ref, o_ref):
    span = WINDOW + QB
    for b in range(tokens // QB):
        start = tokens + b * QB - WINDOW
        keys = k_ref[start:start + span, :]
        values = v_ref[start:start + span, :]
        values = jnp.concatenate([values, jnp.ones_like(values)], axis=1)
        rows = slice(b * QB, (b + 1) * QB)
        q_at = b * QB + lax.broadcasted_iota(jnp.int32, (QB, span), 0)
        k_at = start - tokens + lax.broadcasted_iota(jnp.int32, (QB, span), 1)
        gap = q_at - k_at
        allowed = (k_at + me[0] * tokens >= 0) & (gap >= 0) & (gap < WINDOW)
        for g in range(group):
            scores = dot_t(q_ref[rows, g * HD:(g + 1) * HD], keys)
            out, total, _ = softmax_part(jnp.where(allowed, scores, NONE), values)
            o_ref[rows, g * HD:(g + 1) * HD] = out / total


def local_part(me, queries, keys, values, kv, group):
    tokens = queries.shape[0]
    return pl.pallas_call(
        functools.partial(local_kernel, group, tokens),
        out_shape=jax.ShapeDtypeStruct(queries.shape, jnp.float32),
        grid_spec=pltpu.PrefetchScalarGridSpec(
            num_scalar_prefetch=1,
            grid=(kv,),
            in_specs=[
                pl.BlockSpec((tokens, group * HD), lambda h, m: (0, h)),
                pl.BlockSpec((keys.shape[0], HD), lambda h, m: (0, h)),
                pl.BlockSpec((keys.shape[0], HD), lambda h, m: (0, h)),
            ],
            out_specs=pl.BlockSpec((tokens, group * HD), lambda h, m: (0, h)),
        ),
        compiler_params=pltpu.CompilerParams(vmem_limit_bytes=VMEM_LIMIT),
        cost_estimate=pl.CostEstimate(
            flops=tokens * kv * group * 384 * HD * 6,
            bytes_accessed=tokens * kv * group * HD * 6,
            transcendentals=tokens * kv * group * 384,
        ),
        name="local_part",
    )(me, queries, keys, values)


def level_of(tile):
    x = tile.astype(jnp.float32)
    return x + pltpu.roll(x, LANES - 32, 1) + pltpu.roll(x, LANES - 64, 1)


def merged(parts):
    heads = parts[0].shape[1] // HD - 1
    levels = [level_of(part[:, heads * HD:]) for part in parts]
    top = functools.reduce(jnp.maximum, levels)
    weights = [jnp.exp2(level - top) for level in levels]
    total = functools.reduce(jnp.add, weights)
    shares = [w / total for w in weights]
    outs = []
    for at in range(heads):
        cols = slice(at * HD, (at + 1) * HD)
        terms = [
            part[:, cols].astype(jnp.float32) * share[:, at:at + 1]
            for part, share in zip(parts, shares)
        ]
        outs.append(functools.reduce(jnp.add, terms))
    return outs, top + jnp.log2(total)


def merge_kernel(part_right, part_left, got_right, got_left, right_ref, left_ref):
    for part, got, o_ref in ((part_right, got_right, right_ref), (part_left, got_left, left_ref)):
        outs, level = merged([part, got])
        for at, out in enumerate(outs):
            o_ref[:, at * HD:(at + 1) * HD] = out.astype(jnp.bfloat16)
        o_ref[:, -LANES:] = packed_level(level)


def final_kernel(offset, part_right, part_left, got_right, got_left, local_ref, gate_ref, o_ref):
    outs = merged([part_right, got_right])[0] + merged([part_left, got_left])[0]
    for at, out in enumerate(outs):
        cols = slice(at * HD, (at + 1) * HD)
        share = gate_ref[:, cols]
        o_ref[:, cols] = (share * out + (1.0 - share) * local_ref[:, cols]).astype(jnp.bfloat16)


def merge(part, got):
    tokens, width = got[0].shape
    rows = QB
    spec = pl.BlockSpec((rows, width), lambda r: (r, 0))
    other = pl.BlockSpec((rows, width), lambda r: (r, 1))
    return pl.pallas_call(
        merge_kernel,
        out_shape=[jax.ShapeDtypeStruct(got[0].shape, jnp.bfloat16)] * 2,
        grid=(tokens // rows,),
        in_specs=[spec, other, spec, spec],
        out_specs=[spec] * 2,
        compiler_params=pltpu.CompilerParams(vmem_limit_bytes=VMEM_LIMIT),
        cost_estimate=pl.CostEstimate(
            flops=part.size * 8, bytes_accessed=part.size * 6, transcendentals=tokens * LANES * 8
        ),
        name="merge",
    )(part, part, *got)


def finish(first_row, count, part, got, local, gate):
    width = got[0].shape[1]
    rows = math.gcd(QB, count) if count < QB else QB
    full = local.shape[1]
    spec = pl.BlockSpec((rows, width), lambda r, f: (f[0] + r, 0))
    other = pl.BlockSpec((rows, width), lambda r, f: (f[0] + r, 1))
    return pl.pallas_call(
        final_kernel,
        out_shape=jax.ShapeDtypeStruct((count, full), jnp.bfloat16),
        grid_spec=pltpu.PrefetchScalarGridSpec(
            num_scalar_prefetch=1,
            grid=(count // rows,),
            in_specs=[
                spec, other, spec, spec,
                pl.BlockSpec((rows, full), lambda r, f: (f[0] + r, 0)),
                pl.BlockSpec((1, full), lambda r, f: (0, 0)),
            ],
            out_specs=pl.BlockSpec((rows, full), lambda r, f: (r, 0)),
        ),
        compiler_params=pltpu.CompilerParams(vmem_limit_bytes=VMEM_LIMIT),
        cost_estimate=pl.CostEstimate(
            flops=count * full * 10, bytes_accessed=count * full * 14, transcendentals=count * LANES
        ),
        name="finish",
    )(first_row // rows, part, part, *got, local, gate)


def chip_ring(chips):
    across = 1
    while across * 2 * across * 2 <= chips:
        across *= 2
    deep = chips // across
    walk = []
    for z in range(deep):
        row = range(1, across) if z % 2 == 0 else range(across - 1, 0, -1)
        walk += [z * across + x for x in row]
    return walk + [z * across for z in range(deep - 1, -1, -1)]


def block_tables(block_ids, chips, blocks_chip, cap):
    owner = block_ids // blocks_chip
    inside = block_ids % blocks_chip
    mine = owner[None] == jnp.arange(chips, dtype=jnp.int32)[:, None, None, None]
    count = block_ids.shape[-1]
    earlier = jnp.tril(jnp.ones((count, count), jnp.int32), -1)
    rank = jnp.sum(mine[..., None, :].astype(jnp.int32) * earlier, axis=-1, dtype=jnp.int32)
    picked = mine[..., None, :] & (rank[..., None, :] == jnp.arange(cap, dtype=jnp.int32)[:, None])
    slots = jnp.sum(jnp.where(picked, inside[None, :, :, None, :], 0), axis=-1, dtype=jnp.int32)
    total = jnp.sum(mine, axis=-1, keepdims=True, dtype=jnp.int32)
    return jnp.concatenate([total, slots], axis=-1).reshape(chips, -1)


def to_heads(array):
    if lax.axis_size("head") != 2:
        return lax.all_to_all(array, "head", split_axis=1, concat_axis=0, tiled=True)
    here = lax.axis_index("head")
    width = array.shape[1] // 2
    kept = lax.dynamic_slice_in_dim(array, here * width, width, 1)
    got = lax.ppermute(
        lax.dynamic_slice_in_dim(array, (1 - here) * width, width, 1), "head", [(0, 1), (1, 0)]
    )
    return jnp.concatenate(
        [jnp.where(here == 0, kept, got), jnp.where(here == 0, got, kept)], axis=0
    )


def per_device(
    queries, local_keys, local_values, memory_keys, memory_values, block_ids, mixing_offset_per_head
):
    devices = lax.axis_size("mem")
    me = lax.axis_index("mem")
    chips = devices // 2
    chip, core = me // 2, me % 2
    q_heads = to_heads(queries)
    tokens = q_heads.shape[0]
    kv = block_ids.shape[1]
    heads = q_heads.shape[1] // HD
    group = heads // kv
    half = heads // 2
    right, left = q_heads[:, :half * HD], q_heads[:, half * HD:]

    siblings = [(i, i ^ 1) for i in range(devices)]
    sib_keys, sib_values = (lax.ppermute(x, "mem", siblings) for x in (memory_keys, memory_values))
    keys, values = (memory_keys, sib_keys), (memory_values, sib_values)

    blocks_here = memory_keys.shape[0] // BL
    cap = 2 * ((2 * TOPK + devices - 1) // devices)
    table = block_tables(block_ids, chips, 2 * blocks_here, cap)
    table = lax.all_to_all(
        jnp.repeat(table, 2, axis=0), "mem", split_axis=0, concat_axis=0, tiled=True
    )
    table = table.reshape(-1, 1 + cap)
    swapped = (table + blocks_here) % (2 * blocks_here)
    is_count = jnp.arange(1 + cap) == 0
    table = jnp.where(is_count | (core == 0), table, swapped).reshape(-1)

    ring = chip_ring(chips)
    order = jnp.array(ring, jnp.int32)
    position = jnp.array([ring.index(c) for c in range(chips)], jnp.int32)[chip]
    steps = jnp.arange(chips, dtype=jnp.int32)
    dests = jnp.concatenate([order[(position - steps) % chips], order[(position + steps) % chips]])
    dests = dests * 2 + core
    onward = [
        (ring[i] * 2 + c, ring[(i + 1) % chips] * 2 + c) for i in range(chips) for c in range(2)
    ]
    backward = [(b, a) for a, b in onward]

    def part(step, right, left):
        return memory_part(step, dests, table, right, left, keys, values, kv, cap)

    keys_own, values_own = to_heads(local_keys), to_heads(local_values)
    behind = [(i, i + 1) for i in range(devices - 1)]
    keys_before, values_before = (lax.ppermute(x, "mem", behind) for x in (keys_own, values_own))
    local_out = local_part(
        me.reshape(1).astype(jnp.int32),
        q_heads,
        jnp.concatenate([keys_before, keys_own], axis=0),
        jnp.concatenate([values_before, values_own], axis=0),
        kv,
        group,
    )
    gate = jnp.repeat(jax.nn.sigmoid(mixing_offset_per_head), HD)[None, :]
    own = part(0, right, left)

    got = None
    for step in range(1, chips):
        right = lax.ppermute(right, "mem", onward)
        left = lax.ppermute(left, "mem", backward)
        if step == 2:
            right, left, own, local_out = lax.optimization_barrier((right, left, own, local_out))
        now = part(step, right, left)
        if got is None:
            width = now.shape[1] // 2
            now = now[:, :width], now[:, width:]
        else:
            now = merge(now, got)
        got = lax.ppermute(now[0], "mem", onward), lax.ppermute(now[1], "mem", backward)

    shares = lax.axis_size("head")
    if shares != 2:
        done = finish(jnp.zeros((1,), jnp.int32), tokens, own, got, local_out, gate)
        return lax.all_to_all(done, "head", split_axis=0, concat_axis=1, tiled=True)
    here = lax.axis_index("head").astype(jnp.int32).reshape(1)
    count = tokens // 2
    away = finish((1 - here) * count, count, own, got, local_out, gate)
    back = lax.ppermute(away, "head", [(0, 1), (1, 0)])
    kept = finish(here * count, count, own, got, local_out, gate)
    return jnp.concatenate(
        [jnp.where(here[0] == 0, kept, back), jnp.where(here[0] == 0, back, kept)], axis=1
    )


def solution(mesh):
    return jax.shard_map(
        per_device,
        mesh=mesh,
        in_specs=(
            P(("mem", "head"), None),
            P(("mem", "head"), None),
            P(("mem", "head"), None),
            P("mem", "head"),
            P("mem", "head"),
            P("mem", "head", None),
            P("head"),
        ),
        out_specs=P(("mem", "head"), None),
        check_vma=False,
    )
```

```python
import functools
import math

import jax
import jax.numpy as jnp
from jax import lax
from jax.experimental import pallas as pl
from jax.experimental.pallas import tpu as pltpu
from jax.sharding import PartitionSpec as P

HD = 128
QB = 128
BL = 128
TOPK = 32
WINDOW = 256
LANES = 128
NONE = -1e30
SCALE2 = math.log2(math.e) / math.sqrt(HD)
VMEM_LIMIT = 28 * 1024 * 1024


def dot_t(a, b):
    return lax.dot_general(a, b, (((1,), (1,)), ((), ())), preferred_element_type=jnp.float32)


def lane_of(shape):
    return lax.broadcasted_iota(jnp.int32, shape, 1)


def split3(x):
    hi = x.astype(jnp.bfloat16).astype(jnp.float32)
    rest = x - hi
    mid = rest.astype(jnp.bfloat16).astype(jnp.float32)
    return hi, mid, rest - mid


def packed_level(level):
    lane = lane_of(level.shape)
    hi, mid, low = split3(level)
    stat = jnp.where(lane < 32, hi, 0.0)
    stat = jnp.where((lane >= 32) & (lane < 64), pltpu.roll(mid, 32, 1), stat)
    stat = jnp.where((lane >= 64) & (lane < 96), pltpu.roll(low, 64, 1), stat)
    return stat.astype(jnp.bfloat16)


def softmax_part(scores, values_and_ones):
    top = jnp.max(scores, axis=1, keepdims=True)
    weights = jnp.exp2((scores - top) * SCALE2).astype(jnp.bfloat16)
    both = jnp.dot(weights, values_and_ones, preferred_element_type=jnp.float32)
    return both[:, :HD], both[:, HD:], top


def part_kernel(
    step, chips, group, cap, kv, per_kv, dests, table, right_ref, left_ref, k_ref, k_sib, v_ref, v_sib,
    o_ref, q_ref, top_ref, total_ref
):
    index = pl.program_id(0)
    each = pl.num_programs(0) // 2
    way = index // each
    chunk = dests[way * chips + step]
    tokens = q_ref.shape[0]
    blocks = k_ref.shape[0] // BL
    kv_head = index * group // per_kv
    place0 = index * group + way

    @pl.when(way == 0)
    def _():
        q_ref[...] = right_ref[...]

    @pl.when(way == 1)
    def _():
        q_ref[...] = left_ref[...]

    def one_block(b, carry):
        entry = ((chunk * (tokens // QB) + b) * kv + kv_head) * (1 + cap)
        rows = pl.ds(pl.multiple_of(b * QB, QB), QB)
        count = table[entry]
        lane = lane_of((QB, LANES))

        def put(outs, totals, tops):
            top, total = top_ref[rows, :], total_ref[rows, :]
            for g in range(group):
                o_ref[rows, pl.ds(pl.multiple_of((place0 + g) * HD, HD), HD)] = outs[g].astype(
                    jnp.bfloat16
                )
                here = lane == (index - way * each) * group + g
                top = jnp.where(here, tops[g], top)
                total = jnp.where(here, totals[g], total)
            top_ref[rows, :] = top
            total_ref[rows, :] = total

        def block_of(own, sib, i):
            slot = table[entry + 1 + i]
            inside = pl.multiple_of(lax.rem(slot, blocks) * BL, BL)
            return jnp.where(slot < blocks, own[pl.ds(inside, BL), :], sib[pl.ds(inside, BL), :])

        @pl.when(count == 0)
        def _():
            blank = jnp.zeros((QB, HD), jnp.float32)
            put([blank] * group, [blank + 1.0] * group, [blank + NONE] * group)

        for size in range(1, cap + 1):
            @pl.when(count == size)
            def _(size=size):
                keys = jnp.concatenate([block_of(k_ref, k_sib, i) for i in range(size)], axis=0)
                values = jnp.concatenate([block_of(v_ref, v_sib, i) for i in range(size)], axis=0)
                values = jnp.concatenate([values, jnp.ones_like(values)], axis=1)
                asked = jnp.concatenate(
                    [q_ref[rows, g * HD:(g + 1) * HD] for g in range(group)], axis=0
                )
                out, total, top = softmax_part(dot_t(asked, keys), values)
                out = out / total
                cut = [slice(g * QB, (g + 1) * QB) for g in range(group)]
                put([out[c] for c in cut], [total[c] for c in cut], [top[c] for c in cut])

        return carry

    lax.fori_loop(0, tokens // QB, one_block, 0)

    @pl.when(index == (way + 1) * each - 1)
    def _():
        stat = pl.ds(pl.multiple_of((place0 + group) * HD, HD), HD)
        o_ref[:, stat] = packed_level(top_ref[...] * SCALE2 + jnp.log2(total_ref[...]))


def memory_part(step, dests, table, right, left, keys, values, kv, cap):
    tokens, width = right.shape
    heads = width // HD
    per_kv = 2 * heads // kv
    group = min(per_kv, heads)
    each = heads // group
    chips = dests.shape[0] // 2
    work = 2 * tokens * heads * cap * BL // 2
    of_head = pl.BlockSpec((keys[0].shape[0], HD), lambda i, d, t: (0, i * group // per_kv))
    return pl.pallas_call(
        functools.partial(part_kernel, step, chips, group, cap, kv, per_kv),
        out_shape=jax.ShapeDtypeStruct((tokens, 2 * (width + LANES)), jnp.bfloat16),
        grid_spec=pltpu.PrefetchScalarGridSpec(
            num_scalar_prefetch=2,
            grid=(2 * each,),
            in_specs=[
                pl.BlockSpec((tokens, group * HD), lambda i, d, t: (0, jnp.minimum(i, each - 1))),
                pl.BlockSpec((tokens, group * HD), lambda i, d, t: (0, jnp.maximum(i - each, 0))),
            ] + [of_head] * 4,
            out_specs=pl.BlockSpec((tokens, 2 * (width + LANES)), lambda i, d, t: (0, 0)),
            scratch_shapes=[pltpu.VMEM((tokens, group * HD), jnp.bfloat16)]
            + [pltpu.VMEM((tokens, LANES), jnp.float32)] * 2,
        ),
        compiler_params=pltpu.CompilerParams(vmem_limit_bytes=VMEM_LIMIT),
        cost_estimate=pl.CostEstimate(
            flops=work * HD * 6, bytes_accessed=keys[0].size * 8, transcendentals=work
        ),
        name="memory_part",
    )(dests, table, right, left, *keys, *values)


def local_kernel(group, tokens, me, q_ref, k_ref, v_ref, o_ref):
    span = WINDOW + QB
    for b in range(tokens // QB):
        start = tokens + b * QB - WINDOW
        keys = k_ref[start:start + span, :]
        values = v_ref[start:start + span, :]
        values = jnp.concatenate([values, jnp.ones_like(values)], axis=1)
        rows = slice(b * QB, (b + 1) * QB)
        q_at = b * QB + lax.broadcasted_iota(jnp.int32, (QB, span), 0)
        k_at = start - tokens + lax.broadcasted_iota(jnp.int32, (QB, span), 1)
        gap = q_at - k_at
        allowed = (k_at + me[0] * tokens >= 0) & (gap >= 0) & (gap < WINDOW)
        for g in range(group):
            scores = dot_t(q_ref[rows, g * HD:(g + 1) * HD], keys)
            out, total, _ = softmax_part(jnp.where(allowed, scores, NONE), values)
            o_ref[rows, g * HD:(g + 1) * HD] = out / total


def local_part(me, queries, keys, values, kv, group):
    tokens = queries.shape[0]
    return pl.pallas_call(
        functools.partial(local_kernel, group, tokens),
        out_shape=jax.ShapeDtypeStruct(queries.shape, jnp.float32),
        grid_spec=pltpu.PrefetchScalarGridSpec(
            num_scalar_prefetch=1,
            grid=(kv,),
            in_specs=[
                pl.BlockSpec((tokens, group * HD), lambda h, m: (0, h)),
                pl.BlockSpec((keys.shape[0], HD), lambda h, m: (0, h)),
                pl.BlockSpec((keys.shape[0], HD), lambda h, m: (0, h)),
            ],
            out_specs=pl.BlockSpec((tokens, group * HD), lambda h, m: (0, h)),
        ),
        compiler_params=pltpu.CompilerParams(vmem_limit_bytes=VMEM_LIMIT),
        cost_estimate=pl.CostEstimate(
            flops=tokens * kv * group * 384 * HD * 6,
            bytes_accessed=tokens * kv * group * HD * 6,
            transcendentals=tokens * kv * group * 384,
        ),
        name="local_part",
    )(me, queries, keys, values)


def level_of(tile):
    x = tile.astype(jnp.float32)
    return x + pltpu.roll(x, LANES - 32, 1) + pltpu.roll(x, LANES - 64, 1)


def merged(parts):
    heads = parts[0].shape[1] // HD - 1
    levels = [level_of(part[:, heads * HD:]) for part in parts]
    top = functools.reduce(jnp.maximum, levels)
    weights = [jnp.exp2(level - top) for level in levels]
    total = functools.reduce(jnp.add, weights)
    shares = [w / total for w in weights]
    outs = []
    for at in range(heads):
        cols = slice(at * HD, (at + 1) * HD)
        terms = [
            part[:, cols].astype(jnp.float32) * share[:, at:at + 1]
            for part, share in zip(parts, shares)
        ]
        outs.append(functools.reduce(jnp.add, terms))
    return outs, top + jnp.log2(total)


def merge_kernel(part_right, part_left, got_right, got_left, right_ref, left_ref):
    for part, got, o_ref in ((part_right, got_right, right_ref), (part_left, got_left, left_ref)):
        outs, level = merged([part, got])
        for at, out in enumerate(outs):
            o_ref[:, at * HD:(at + 1) * HD] = out.astype(jnp.bfloat16)
        o_ref[:, -LANES:] = packed_level(level)


def final_kernel(offset, part_right, part_left, got_right, got_left, local_ref, gate_ref, o_ref):
    outs = merged([part_right, got_right])[0] + merged([part_left, got_left])[0]
    for at, out in enumerate(outs):
        cols = slice(at * HD, (at + 1) * HD)
        share = gate_ref[:, cols]
        o_ref[:, cols] = (share * out + (1.0 - share) * local_ref[:, cols]).astype(jnp.bfloat16)


def merge(part, got):
    tokens, width = got[0].shape
    rows = QB
    spec = pl.BlockSpec((rows, width), lambda r: (r, 0))
    other = pl.BlockSpec((rows, width), lambda r: (r, 1))
    return pl.pallas_call(
        merge_kernel,
        out_shape=[jax.ShapeDtypeStruct(got[0].shape, jnp.bfloat16)] * 2,
        grid=(tokens // rows,),
        in_specs=[spec, other, spec, spec],
        out_specs=[spec] * 2,
        compiler_params=pltpu.CompilerParams(vmem_limit_bytes=VMEM_LIMIT),
        cost_estimate=pl.CostEstimate(
            flops=part.size * 8, bytes_accessed=part.size * 6, transcendentals=tokens * LANES * 8
        ),
        name="merge",
    )(part, part, *got)


def finish(first_row, count, part, got, local, gate):
    width = got[0].shape[1]
    rows = math.gcd(QB, count) if count < QB else QB
    full = local.shape[1]
    spec = pl.BlockSpec((rows, width), lambda r, f: (f[0] + r, 0))
    other = pl.BlockSpec((rows, width), lambda r, f: (f[0] + r, 1))
    return pl.pallas_call(
        final_kernel,
        out_shape=jax.ShapeDtypeStruct((count, full), jnp.bfloat16),
        grid_spec=pltpu.PrefetchScalarGridSpec(
            num_scalar_prefetch=1,
            grid=(count // rows,),
            in_specs=[
                spec, other, spec, spec,
                pl.BlockSpec((rows, full), lambda r, f: (f[0] + r, 0)),
                pl.BlockSpec((1, full), lambda r, f: (0, 0)),
            ],
            out_specs=pl.BlockSpec((rows, full), lambda r, f: (r, 0)),
        ),
        compiler_params=pltpu.CompilerParams(vmem_limit_bytes=VMEM_LIMIT),
        cost_estimate=pl.CostEstimate(
            flops=count * full * 10, bytes_accessed=count * full * 14, transcendentals=count * LANES
        ),
        name="finish",
    )(first_row // rows, part, part, *got, local, gate)


def chip_ring(chips):
    across = 1
    while across * 2 * across * 2 <= chips:
        across *= 2
    deep = chips // across
    walk = []
    for z in range(deep):
        row = range(1, across) if z % 2 == 0 else range(across - 1, 0, -1)
        walk += [z * across + x for x in row]
    return walk + [z * across for z in range(deep - 1, -1, -1)]


def block_tables(block_ids, chips, blocks_chip, cap):
    owner = block_ids // blocks_chip
    inside = block_ids % blocks_chip
    mine = owner[None] == jnp.arange(chips, dtype=jnp.int32)[:, None, None, None]
    count = block_ids.shape[-1]
    earlier = jnp.tril(jnp.ones((count, count), jnp.int32), -1)
    rank = jnp.sum(mine[..., None, :].astype(jnp.int32) * earlier, axis=-1, dtype=jnp.int32)
    picked = mine[..., None, :] & (rank[..., None, :] == jnp.arange(cap, dtype=jnp.int32)[:, None])
    slots = jnp.sum(jnp.where(picked, inside[None, :, :, None, :], 0), axis=-1, dtype=jnp.int32)
    total = jnp.sum(mine, axis=-1, keepdims=True, dtype=jnp.int32)
    return jnp.concatenate([total, slots], axis=-1).reshape(chips, -1)


def to_heads(array):
    if lax.axis_size("head") != 2:
        return lax.all_to_all(array, "head", split_axis=1, concat_axis=0, tiled=True)
    here = lax.axis_index("head")
    width = array.shape[1] // 2
    kept = lax.dynamic_slice_in_dim(array, here * width, width, 1)
    got = lax.ppermute(
        lax.dynamic_slice_in_dim(array, (1 - here) * width, width, 1), "head", [(0, 1), (1, 0)]
    )
    return jnp.concatenate(
        [jnp.where(here == 0, kept, got), jnp.where(here == 0, got, kept)], axis=0
    )


def per_device(
    queries, local_keys, local_values, memory_keys, memory_values, block_ids, mixing_offset_per_head
):
    devices = lax.axis_size("mem")
    me = lax.axis_index("mem")
    chips = devices // 2
    chip, core = me // 2, me % 2
    q_heads = to_heads(queries)
    tokens = q_heads.shape[0]
    kv = block_ids.shape[1]
    heads = q_heads.shape[1] // HD
    group = heads // kv
    half = heads // 2
    right, left = q_heads[:, :half * HD], q_heads[:, half * HD:]

    siblings = [(i, i ^ 1) for i in range(devices)]
    sib_keys, sib_values = (lax.ppermute(x, "mem", siblings) for x in (memory_keys, memory_values))
    keys, values = (memory_keys, sib_keys), (memory_values, sib_values)

    blocks_here = memory_keys.shape[0] // BL
    cap = 2 * ((2 * TOPK + devices - 1) // devices)
    table = block_tables(block_ids, chips, 2 * blocks_here, cap)
    right, left, table = lax.optimization_barrier((right, left, table))
    table = lax.all_to_all(
        jnp.repeat(table, 2, axis=0), "mem", split_axis=0, concat_axis=0, tiled=True
    )
    table = table.reshape(-1, 1 + cap)
    swapped = (table + blocks_here) % (2 * blocks_here)
    is_count = jnp.arange(1 + cap) == 0
    table = jnp.where(is_count | (core == 0), table, swapped).reshape(-1)

    ring = chip_ring(chips)
    order = jnp.array(ring, jnp.int32)
    position = jnp.array([ring.index(c) for c in range(chips)], jnp.int32)[chip]
    steps = jnp.arange(chips, dtype=jnp.int32)
    dests = jnp.concatenate([order[(position - steps) % chips], order[(position + steps) % chips]])
    dests = dests * 2 + core
    onward = [
        (ring[i] * 2 + c, ring[(i + 1) % chips] * 2 + c) for i in range(chips) for c in range(2)
    ]
    backward = [(b, a) for a, b in onward]

    def part(step, right, left):
        return memory_part(step, dests, table, right, left, keys, values, kv, cap)

    keys_own, values_own = to_heads(local_keys), to_heads(local_values)
    behind = [(i, i + 1) for i in range(devices - 1)]
    keys_before, values_before = (lax.ppermute(x, "mem", behind) for x in (keys_own, values_own))
    local_out = local_part(
        me.reshape(1).astype(jnp.int32),
        q_heads,
        jnp.concatenate([keys_before, keys_own], axis=0),
        jnp.concatenate([values_before, values_own], axis=0),
        kv,
        group,
    )
    gate = jnp.repeat(jax.nn.sigmoid(mixing_offset_per_head), HD)[None, :]
    own = part(0, right, left)

    def hop(right, left):
        return lax.ppermute(right, "mem", onward), lax.ppermute(left, "mem", backward)

    asked = [(right, left), hop(right, left)]
    got = None
    for step in range(1, chips):
        if step + 1 < chips:
            asked.append(hop(*asked[step]))
        mine = asked[step]
        if step == 2:
            mine, local_out = lax.optimization_barrier((mine, local_out))
        now = part(step, *mine)
        if got is None:
            width = now.shape[1] // 2
            now = now[:, :width], now[:, width:]
        else:
            now = merge(now, got)
        got = hop(*now)

    shares = lax.axis_size("head")
    if shares != 2:
        done = finish(jnp.zeros((1,), jnp.int32), tokens, own, got, local_out, gate)
        return lax.all_to_all(done, "head", split_axis=0, concat_axis=1, tiled=True)
    here = lax.axis_index("head").astype(jnp.int32).reshape(1)
    count = tokens // 2
    away = finish((1 - here) * count, count, own, got, local_out, gate)
    back = lax.ppermute(away, "head", [(0, 1), (1, 0)])
    kept = finish(here * count, count, own, got, local_out, gate)
    return jnp.concatenate(
        [jnp.where(here[0] == 0, kept, back), jnp.where(here[0] == 0, back, kept)], axis=1
    )


def solution(mesh):
    return jax.shard_map(
        per_device,
        mesh=mesh,
        in_specs=(
            P(("mem", "head"), None),
            P(("mem", "head"), None),
            P(("mem", "head"), None),
            P("mem", "head"),
            P("mem", "head"),
            P("mem", "head", None),
            P("head"),
        ),
        out_specs=P(("mem", "head"), None),
        check_vma=False,
    )
```

```python
import functools
import math

import jax
import jax.numpy as jnp
from jax import lax
from jax.experimental import pallas as pl
from jax.experimental.pallas import tpu as pltpu
from jax.sharding import PartitionSpec as P

HD = 128
QB = 128
BL = 128
TOPK = 32
WINDOW = 256
LANES = 128
NONE = -1e30
SCALE2 = math.log2(math.e) / math.sqrt(HD)
VMEM_LIMIT = 28 * 1024 * 1024


def dot_t(a, b):
    return lax.dot_general(a, b, (((1,), (1,)), ((), ())), preferred_element_type=jnp.float32)


def lane_of(shape):
    return lax.broadcasted_iota(jnp.int32, shape, 1)


def split3(x):
    hi = x.astype(jnp.bfloat16).astype(jnp.float32)
    rest = x - hi
    mid = rest.astype(jnp.bfloat16).astype(jnp.float32)
    return hi, mid, rest - mid


def packed_level(level):
    lane = lane_of(level.shape)
    hi, mid, low = split3(level)
    stat = jnp.where(lane < 32, hi, 0.0)
    stat = jnp.where((lane >= 32) & (lane < 64), pltpu.roll(mid, 32, 1), stat)
    stat = jnp.where((lane >= 64) & (lane < 96), pltpu.roll(low, 64, 1), stat)
    return stat.astype(jnp.bfloat16)


def softmax_part(scores, values_and_ones):
    top = jnp.max(scores, axis=1, keepdims=True)
    weights = jnp.exp2((scores - top) * SCALE2).astype(jnp.bfloat16)
    both = jnp.dot(weights, values_and_ones, preferred_element_type=jnp.float32)
    return both[:, :HD], both[:, HD:], top


def part_kernel(
    step, chips, group, cap, kv, per_kv, dests, table, right_ref, left_ref, k_ref, k_sib, v_ref, v_sib,
    o_ref, q_ref, top_ref, total_ref
):
    index = pl.program_id(0)
    each = pl.num_programs(0) // 2
    way = index // each
    chunk = dests[way * chips + step]
    tokens = q_ref.shape[0]
    blocks = k_ref.shape[0] // BL
    kv_head = index * group // per_kv
    place0 = index * group + way

    @pl.when(way == 0)
    def _():
        q_ref[...] = right_ref[...]

    @pl.when(way == 1)
    def _():
        q_ref[...] = left_ref[...]

    def one_block(b, carry):
        entry = ((chunk * (tokens // QB) + b) * kv + kv_head) * (1 + cap)
        rows = pl.ds(pl.multiple_of(b * QB, QB), QB)
        count = table[entry]
        lane = lane_of((QB, LANES))

        def put(outs, totals, tops):
            top, total = top_ref[rows, :], total_ref[rows, :]
            for g in range(group):
                o_ref[rows, pl.ds(pl.multiple_of((place0 + g) * HD, HD), HD)] = outs[g].astype(
                    jnp.bfloat16
                )
                here = lane == (index - way * each) * group + g
                top = jnp.where(here, tops[g], top)
                total = jnp.where(here, totals[g], total)
            top_ref[rows, :] = top
            total_ref[rows, :] = total

        def block_of(own, sib, i):
            slot = table[entry + 1 + i]
            inside = pl.multiple_of(lax.rem(slot, blocks) * BL, BL)
            return jnp.where(slot < blocks, own[pl.ds(inside, BL), :], sib[pl.ds(inside, BL), :])

        @pl.when(count == 0)
        def _():
            blank = jnp.zeros((QB, HD), jnp.float32)
            put([blank] * group, [blank + 1.0] * group, [blank + NONE] * group)

        for size in range(1, cap + 1):
            @pl.when(count == size)
            def _(size=size):
                keys = jnp.concatenate([block_of(k_ref, k_sib, i) for i in range(size)], axis=0)
                values = jnp.concatenate([block_of(v_ref, v_sib, i) for i in range(size)], axis=0)
                values = jnp.concatenate([values, jnp.ones_like(values)], axis=1)
                asked = jnp.concatenate(
                    [q_ref[rows, g * HD:(g + 1) * HD] for g in range(group)], axis=0
                )
                out, total, top = softmax_part(dot_t(asked, keys), values)
                out = out / total
                cut = [slice(g * QB, (g + 1) * QB) for g in range(group)]
                put([out[c] for c in cut], [total[c] for c in cut], [top[c] for c in cut])

        return carry

    lax.fori_loop(0, tokens // QB, one_block, 0)

    @pl.when(index == (way + 1) * each - 1)
    def _():
        stat = pl.ds(pl.multiple_of((place0 + group) * HD, HD), HD)
        o_ref[:, stat] = packed_level(top_ref[...] * SCALE2 + jnp.log2(total_ref[...]))


def memory_part(step, dests, table, right, left, keys, values, kv, cap):
    tokens, width = right.shape
    heads = width // HD
    per_kv = 2 * heads // kv
    group = min(per_kv, heads)
    each = heads // group
    chips = dests.shape[0] // 2
    work = 2 * tokens * heads * cap * BL // 2
    of_head = pl.BlockSpec((keys[0].shape[0], HD), lambda i, d, t: (0, i * group // per_kv))
    return pl.pallas_call(
        functools.partial(part_kernel, step, chips, group, cap, kv, per_kv),
        out_shape=jax.ShapeDtypeStruct((tokens, 2 * (width + LANES)), jnp.bfloat16),
        grid_spec=pltpu.PrefetchScalarGridSpec(
            num_scalar_prefetch=2,
            grid=(2 * each,),
            in_specs=[
                pl.BlockSpec((tokens, group * HD), lambda i, d, t: (0, jnp.minimum(i, each - 1))),
                pl.BlockSpec((tokens, group * HD), lambda i, d, t: (0, jnp.maximum(i - each, 0))),
            ] + [of_head] * 4,
            out_specs=pl.BlockSpec((tokens, 2 * (width + LANES)), lambda i, d, t: (0, 0)),
            scratch_shapes=[pltpu.VMEM((tokens, group * HD), jnp.bfloat16)]
            + [pltpu.VMEM((tokens, LANES), jnp.float32)] * 2,
        ),
        compiler_params=pltpu.CompilerParams(vmem_limit_bytes=VMEM_LIMIT),
        cost_estimate=pl.CostEstimate(
            flops=work * HD * 6, bytes_accessed=keys[0].size * 8, transcendentals=work
        ),
        name="memory_part",
    )(dests, table, right, left, *keys, *values)


def local_kernel(group, tokens, me, q_ref, k_ref, v_ref, o_ref):
    span = WINDOW + QB
    for b in range(tokens // QB):
        start = tokens + b * QB - WINDOW
        keys = k_ref[start:start + span, :]
        values = v_ref[start:start + span, :]
        values = jnp.concatenate([values, jnp.ones_like(values)], axis=1)
        rows = slice(b * QB, (b + 1) * QB)
        q_at = b * QB + lax.broadcasted_iota(jnp.int32, (QB, span), 0)
        k_at = start - tokens + lax.broadcasted_iota(jnp.int32, (QB, span), 1)
        gap = q_at - k_at
        allowed = (k_at + me[0] * tokens >= 0) & (gap >= 0) & (gap < WINDOW)
        for g in range(group):
            scores = dot_t(q_ref[rows, g * HD:(g + 1) * HD], keys)
            out, total, _ = softmax_part(jnp.where(allowed, scores, NONE), values)
            o_ref[rows, g * HD:(g + 1) * HD] = out / total


def local_part(me, queries, keys, values, kv, group):
    tokens = queries.shape[0]
    return pl.pallas_call(
        functools.partial(local_kernel, group, tokens),
        out_shape=jax.ShapeDtypeStruct(queries.shape, jnp.float32),
        grid_spec=pltpu.PrefetchScalarGridSpec(
            num_scalar_prefetch=1,
            grid=(kv,),
            in_specs=[
                pl.BlockSpec((tokens, group * HD), lambda h, m: (0, h)),
                pl.BlockSpec((keys.shape[0], HD), lambda h, m: (0, h)),
                pl.BlockSpec((keys.shape[0], HD), lambda h, m: (0, h)),
            ],
            out_specs=pl.BlockSpec((tokens, group * HD), lambda h, m: (0, h)),
        ),
        compiler_params=pltpu.CompilerParams(vmem_limit_bytes=VMEM_LIMIT),
        cost_estimate=pl.CostEstimate(
            flops=tokens * kv * group * 384 * HD * 6,
            bytes_accessed=tokens * kv * group * HD * 6,
            transcendentals=tokens * kv * group * 384,
        ),
        name="local_part",
    )(me, queries, keys, values)


def level_of(tile):
    x = tile.astype(jnp.float32)
    return x + pltpu.roll(x, LANES - 32, 1) + pltpu.roll(x, LANES - 64, 1)


def merged(parts):
    heads = parts[0].shape[1] // HD - 1
    levels = [level_of(part[:, heads * HD:]) for part in parts]
    top = functools.reduce(jnp.maximum, levels)
    weights = [jnp.exp2(level - top) for level in levels]
    total = functools.reduce(jnp.add, weights)
    shares = [w / total for w in weights]
    outs = []
    for at in range(heads):
        cols = slice(at * HD, (at + 1) * HD)
        terms = [
            part[:, cols].astype(jnp.float32) * share[:, at:at + 1]
            for part, share in zip(parts, shares)
        ]
        outs.append(functools.reduce(jnp.add, terms))
    return outs, top + jnp.log2(total)


def merge_kernel(part_right, part_left, got_right, got_left, right_ref, left_ref):
    for part, got, o_ref in ((part_right, got_right, right_ref), (part_left, got_left, left_ref)):
        outs, level = merged([part, got])
        for at, out in enumerate(outs):
            o_ref[:, at * HD:(at + 1) * HD] = out.astype(jnp.bfloat16)
        o_ref[:, -LANES:] = packed_level(level)


def final_kernel(offset, part_right, part_left, got_right, got_left, local_ref, gate_ref, o_ref):
    outs = merged([part_right, got_right])[0] + merged([part_left, got_left])[0]
    for at, out in enumerate(outs):
        cols = slice(at * HD, (at + 1) * HD)
        share = gate_ref[:, cols]
        o_ref[:, cols] = (share * out + (1.0 - share) * local_ref[:, cols]).astype(jnp.bfloat16)


def merge(part, got):
    tokens, width = got[0].shape
    rows = QB
    spec = pl.BlockSpec((rows, width), lambda r: (r, 0))
    other = pl.BlockSpec((rows, width), lambda r: (r, 1))
    return pl.pallas_call(
        merge_kernel,
        out_shape=[jax.ShapeDtypeStruct(got[0].shape, jnp.bfloat16)] * 2,
        grid=(tokens // rows,),
        in_specs=[spec, other, spec, spec],
        out_specs=[spec] * 2,
        compiler_params=pltpu.CompilerParams(vmem_limit_bytes=VMEM_LIMIT),
        cost_estimate=pl.CostEstimate(
            flops=part.size * 8, bytes_accessed=part.size * 6, transcendentals=tokens * LANES * 8
        ),
        name="merge",
    )(part, part, *got)


def finish(first_row, count, part, got, local, gate):
    width = got[0].shape[1]
    rows = math.gcd(QB, count) if count < QB else QB
    full = local.shape[1]
    spec = pl.BlockSpec((rows, width), lambda r, f: (f[0] + r, 0))
    other = pl.BlockSpec((rows, width), lambda r, f: (f[0] + r, 1))
    return pl.pallas_call(
        final_kernel,
        out_shape=jax.ShapeDtypeStruct((count, full), jnp.bfloat16),
        grid_spec=pltpu.PrefetchScalarGridSpec(
            num_scalar_prefetch=1,
            grid=(count // rows,),
            in_specs=[
                spec, other, spec, spec,
                pl.BlockSpec((rows, full), lambda r, f: (f[0] + r, 0)),
                pl.BlockSpec((1, full), lambda r, f: (0, 0)),
            ],
            out_specs=pl.BlockSpec((rows, full), lambda r, f: (r, 0)),
        ),
        compiler_params=pltpu.CompilerParams(vmem_limit_bytes=VMEM_LIMIT),
        cost_estimate=pl.CostEstimate(
            flops=count * full * 10, bytes_accessed=count * full * 14, transcendentals=count * LANES
        ),
        name="finish",
    )(first_row // rows, part, part, *got, local, gate)


def chip_ring(chips):
    across = 1
    while across * 2 * across * 2 <= chips:
        across *= 2
    deep = chips // across
    walk = []
    for z in range(deep):
        row = range(1, across) if z % 2 == 0 else range(across - 1, 0, -1)
        walk += [z * across + x for x in row]
    return walk + [z * across for z in range(deep - 1, -1, -1)]


def block_tables(block_ids, chips, blocks_chip, cap):
    owner = block_ids // blocks_chip
    inside = block_ids % blocks_chip
    mine = owner[None] == jnp.arange(chips, dtype=jnp.int32)[:, None, None, None]
    count = block_ids.shape[-1]
    earlier = jnp.tril(jnp.ones((count, count), jnp.int32), -1)
    rank = jnp.sum(mine[..., None, :].astype(jnp.int32) * earlier, axis=-1, dtype=jnp.int32)
    picked = mine[..., None, :] & (rank[..., None, :] == jnp.arange(cap, dtype=jnp.int32)[:, None])
    slots = jnp.sum(jnp.where(picked, inside[None, :, :, None, :], 0), axis=-1, dtype=jnp.int32)
    total = jnp.sum(mine, axis=-1, keepdims=True, dtype=jnp.int32)
    return jnp.concatenate([total, slots], axis=-1).reshape(chips, -1)


def to_heads(array):
    if lax.axis_size("head") != 2:
        return lax.all_to_all(array, "head", split_axis=1, concat_axis=0, tiled=True)
    here = lax.axis_index("head")
    width = array.shape[1] // 2
    kept = lax.dynamic_slice_in_dim(array, here * width, width, 1)
    got = lax.ppermute(
        lax.dynamic_slice_in_dim(array, (1 - here) * width, width, 1), "head", [(0, 1), (1, 0)]
    )
    return jnp.concatenate(
        [jnp.where(here == 0, kept, got), jnp.where(here == 0, got, kept)], axis=0
    )


def per_device(
    queries, local_keys, local_values, memory_keys, memory_values, block_ids, mixing_offset_per_head
):
    devices = lax.axis_size("mem")
    me = lax.axis_index("mem")
    chips = devices // 2
    chip, core = me // 2, me % 2
    q_heads = to_heads(queries)
    tokens = q_heads.shape[0]
    kv = block_ids.shape[1]
    heads = q_heads.shape[1] // HD
    group = heads // kv
    half = heads // 2
    right, left = q_heads[:, :half * HD], q_heads[:, half * HD:]

    siblings = [(i, i ^ 1) for i in range(devices)]
    sib_keys, sib_values = (lax.ppermute(x, "mem", siblings) for x in (memory_keys, memory_values))
    keys, values = (memory_keys, sib_keys), (memory_values, sib_values)

    blocks_here = memory_keys.shape[0] // BL
    cap = 2 * ((2 * TOPK + devices - 1) // devices)
    table = block_tables(block_ids, chips, 2 * blocks_here, cap)
    right, left, table, local_keys, local_values = lax.optimization_barrier(
        (right, left, table, local_keys, local_values)
    )
    table = lax.all_to_all(
        jnp.repeat(table, 2, axis=0), "mem", split_axis=0, concat_axis=0, tiled=True
    )
    table = table.reshape(-1, 1 + cap)
    swapped = (table + blocks_here) % (2 * blocks_here)
    is_count = jnp.arange(1 + cap) == 0
    table = jnp.where(is_count | (core == 0), table, swapped).reshape(-1)

    ring = chip_ring(chips)
    order = jnp.array(ring, jnp.int32)
    position = jnp.array([ring.index(c) for c in range(chips)], jnp.int32)[chip]
    steps = jnp.arange(chips, dtype=jnp.int32)
    dests = jnp.concatenate([order[(position - steps) % chips], order[(position + steps) % chips]])
    dests = dests * 2 + core
    onward = [
        (ring[i] * 2 + c, ring[(i + 1) % chips] * 2 + c) for i in range(chips) for c in range(2)
    ]
    backward = [(b, a) for a, b in onward]

    def part(step, right, left):
        return memory_part(step, dests, table, right, left, keys, values, kv, cap)

    keys_own, values_own = to_heads(local_keys), to_heads(local_values)
    behind = [(i, i + 1) for i in range(devices - 1)]
    keys_before, values_before = (lax.ppermute(x, "mem", behind) for x in (keys_own, values_own))
    local_out = local_part(
        me.reshape(1).astype(jnp.int32),
        q_heads,
        jnp.concatenate([keys_before, keys_own], axis=0),
        jnp.concatenate([values_before, values_own], axis=0),
        kv,
        group,
    )
    gate = jnp.repeat(jax.nn.sigmoid(mixing_offset_per_head), HD)[None, :]
    own = part(0, right, left)

    def hop(right, left):
        return lax.ppermute(right, "mem", onward), lax.ppermute(left, "mem", backward)

    asked = [(right, left), hop(right, left)]
    got = None
    for step in range(1, chips):
        if step + 1 < chips:
            asked.append(hop(*asked[step]))
        mine = asked[step]
        if step == 2:
            mine, local_out = lax.optimization_barrier((mine, local_out))
        now = part(step, *mine)
        if got is None:
            width = now.shape[1] // 2
            now = now[:, :width], now[:, width:]
        else:
            now = merge(now, got)
        got = hop(*now)

    shares = lax.axis_size("head")
    if shares != 2:
        done = finish(jnp.zeros((1,), jnp.int32), tokens, own, got, local_out, gate)
        return lax.all_to_all(done, "head", split_axis=0, concat_axis=1, tiled=True)
    here = lax.axis_index("head").astype(jnp.int32).reshape(1)
    count = tokens // 2
    away = finish((1 - here) * count, count, own, got, local_out, gate)
    back = lax.ppermute(away, "head", [(0, 1), (1, 0)])
    kept = finish(here * count, count, own, got, local_out, gate)
    return jnp.concatenate(
        [jnp.where(here[0] == 0, kept, back), jnp.where(here[0] == 0, back, kept)], axis=1
    )


def solution(mesh):
    return jax.shard_map(
        per_device,
        mesh=mesh,
        in_specs=(
            P(("mem", "head"), None),
            P(("mem", "head"), None),
            P(("mem", "head"), None),
            P("mem", "head"),
            P("mem", "head"),
            P("mem", "head", None),
            P("head"),
        ),
        out_specs=P(("mem", "head"), None),
        check_vma=False,
    )
```
